512 devices in a mesh: row: 16 (over y_hi, x, core), col: 16 (over z), vir: 2 (over y_lo).
Axes of the slice: x: 4, y: 4 (y_hi: 2, y_lo: 2; y = y_hi * 2 + y_lo), z: 16, core: 2. Of those that a mesh axis runs over, the one named last changes fastest.
Arguments:
- amplitudes: bfloat16 [32, 32, 512, 512], P('row', 'col', None, 'vir'), may hold values from -6 to 6
- integrals: bfloat16 [32, 32, 512, 512], P('row', 'col', 'vir'), may hold values from -0.15625 to 0.15625
- occ_irrep: int32 [32], replicated, may hold values from 0 to 7, as said below
- vir_irrep: int32 [512], replicated, may hold values from 0 to 7, as said below
Outputs:
- residual: float32 [32, 32, 512, 512], P('row', 'col', None, 'vir')
The draws below stay inside these ranges and needn't reach their ends.
Inputs may be any that keep to these rules, and one draw needn't show every extreme that they name: `occ_irrep`: each of the 8 labels occurs among the occupied orbitals. `vir_irrep`: each of the 8 labels occurs among the virtual orbitals.
All inputs are finite; a program needn't handle non-finite values.
Results may differ from the reference program's by a relative error of at most 0.0052.
Values may be sent and summed in bfloat16 or wider, within the bound.
A program may use at most 64 MiB of HBM per device.

```python
import jax
import jax.numpy as jnp
from jax import lax

OB = 2
NV = 512
NOCC = 32


def irrep_labels(key, count, constant_tag):
    own_key = jax.random.fold_in(key, constant_tag)
    labels = jax.random.randint(own_key, (count,), 0, 8, dtype=jnp.int32)
    positions = jax.random.permutation(jax.random.fold_in(own_key, 1), count)[:8]
    return labels.at[positions].set(jnp.arange(8, dtype=jnp.int32))


def draw_occ_irrep(key, part):
    return irrep_labels(key, NOCC, 11)


def draw_vir_irrep(key, part):
    return irrep_labels(key, NV, 13)


def block_scale(key, extent, split, smallest, largest):
    def one(axis_at, parts):
        heights = jax.random.uniform(jax.random.fold_in(jax.random.fold_in(key, 6), axis_at), (parts,), jnp.float32, smallest / len(split), largest / len(split))
        return jnp.repeat(jnp.exp(heights), extent[axis_at] // parts).reshape((-1,) + (1,) * (len(extent) - axis_at - 1))

    level = one(*split[0])
    for cut in split[1:]:
        level = level * one(*cut)
    return level


def bell_draw(key, shape, scale, most, cuts=(), kind=jnp.bfloat16):
    loudness = block_scale(key, shape, cuts, -0.22, 0.18) if cuts else 1.0
    array = jax.random.normal(key, shape, jnp.float32) * scale * loudness
    return jnp.minimum(jnp.maximum(array, -most), most).astype(kind)


def setup_inputs(seed: int = 0) -> dict:
    splits = jax.random.split(jax.random.key(seed), 5)
    amplitudes = bell_draw(splits[0], (NOCC, NOCC, NV, NV), 1.0, 6.0, ((0, 16), (1, 16), (3, 2)))
    integrals = bell_draw(splits[1], (NOCC, NOCC, NV, NV), (5 * OB * NV // 4) ** -0.5, 0.15625, ((0, 16), (1, 16), (2, 2)))
    occ_irrep = draw_occ_irrep(jax.random.fold_in(splits[4], 71), 0)
    vir_irrep = draw_vir_irrep(jax.random.fold_in(splits[4], 71), 0)
    return dict(amplitudes=amplitudes, integrals=integrals, occ_irrep=occ_irrep, vir_irrep=vir_irrep)


def symmetry_mask(left, right, first, second):
    return (left[:, None, None, None] ^ right[None, :, None, None] ^ first[None, None, :, None] ^ second[None, None, None, :]) == 0


def reference(amplitudes, integrals, occ_irrep, vir_irrep):
    blocks = NOCC // OB
    half_count = NV // 2

    def take_tile(values, first_block, second_block):
        first_start = (first_block * OB).astype(jnp.int32)
        second_start = (second_block * OB).astype(jnp.int32)
        zero_start = jnp.int32(0)
        return lax.dynamic_slice(values, (first_start, second_start, zero_start, zero_start), (OB, OB, NV, NV))

    def block_labels(index):
        return lax.dynamic_slice_in_dim(occ_irrep, (index * OB).astype(jnp.int32), OB)

    def amp_tile(first_block, second_block):
        raw = take_tile(amplitudes, first_block, second_block)
        allowed = symmetry_mask(block_labels(first_block), block_labels(second_block), vir_irrep, vir_irrep)
        masked = jnp.where(allowed, raw, jnp.zeros_like(raw)).astype(jnp.float32)
        return (2.0 * masked - jnp.transpose(masked, (0, 1, 3, 2))).astype(jnp.bfloat16)

    def int_tile(first_block, second_block):
        raw = take_tile(integrals, first_block, second_block)
        allowed = symmetry_mask(block_labels(first_block), block_labels(second_block), vir_irrep, vir_irrep)
        return jnp.where(allowed, raw, jnp.zeros_like(raw))

    def contract(left, right):
        return jnp.einsum("ikac,kjcb->ijab", left.astype(jnp.float32), right.astype(jnp.float32),
                          precision=lax.Precision.HIGHEST, preferred_element_type=jnp.float32)

    def pair_block(index):
        first_block = (index // blocks).astype(jnp.int32)
        second_block = (index % blocks).astype(jnp.int32)
        amp_diag = amp_tile(first_block, first_block)
        amp_own = amp_tile(first_block, second_block)
        int_own = int_tile(first_block, second_block)
        int_diag = int_tile(second_block, second_block)
        total = jnp.zeros((OB, OB, NV, NV), jnp.float32)
        for half in range(2):
            low_edge = half * half_count
            high_edge = low_edge + half_count
            term = contract(amp_diag[:, :, :, low_edge:high_edge], int_own[:, :, low_edge:high_edge, :])
            extra = contract(amp_own[:, :, :, low_edge:high_edge], int_diag[:, :, low_edge:high_edge, :])
            term = term + jnp.where(first_block != second_block, extra, jnp.zeros_like(extra))
            rounded = lax.optimization_barrier(term.astype(jnp.bfloat16))
            total = total + rounded.astype(jnp.float32)
        return total.astype(jnp.bfloat16)

    pieces = lax.map(pair_block, jnp.arange(blocks * blocks, dtype=jnp.int32))
    cycle = pieces.reshape(blocks, blocks, OB, OB, NV, NV).transpose(0, 2, 1, 3, 4, 5).reshape(NOCC, NOCC, NV, NV)
    return cycle.astype(jnp.float32) + jnp.transpose(cycle, (1, 0, 3, 2)).astype(jnp.float32)
```

```python
import functools

import jax
import jax.numpy as jnp
from jax import lax
from jax.experimental import pallas as pl
from jax.experimental.pallas import tpu as pltpu
from jax.sharding import PartitionSpec as P

MESH = pl.DeviceIdType.MESH
LABELS = 8
SLOTS = 48
F32 = jnp.float32
BF16 = jnp.bfloat16

COL_TREE = (
    {0: 4, 4: 8, 8: 7, 12: 11, 11: 10, 5: 6, 3: 2, 15: 14},
    {0: 12, 4: 5, 8: 9, 12: 13},
    {0: 1, 4: 3},
    {0: 15},
)


def lookup(key, table, default):
    found = jnp.int32(default)
    for at, value in table.items():
        found = jnp.where(key == at, jnp.int32(value), found)
    return found


def dot(left, right, left_dim, right_dim):
    return lax.dot_general(left, right, (((left_dim,), (right_dim,)), ((), ())), preferred_element_type=F32)


def remote(src, dst, send_sem, recv_sem, device):
    return pltpu.make_async_remote_copy(
        src_ref=src, dst_ref=dst, send_sem=send_sem, recv_sem=recv_sem, device_id=device, device_id_type=MESH
    )


def column_of(row_labels):
    return jnp.broadcast_to(row_labels, (128, row_labels.shape[1])).T[:, :1]


def slot_matrix(labels, slots):
    count = labels.shape[1]
    is_label = (lax.broadcasted_iota(jnp.int32, (LABELS, count), 0) == labels).astype(F32)
    earlier = (
        lax.broadcasted_iota(jnp.int32, (count, count), 0) < lax.broadcasted_iota(jnp.int32, (count, count), 1)
    ).astype(F32)
    before = dot(is_label.astype(BF16), earlier.astype(BF16), 1, 0)
    rank = jnp.sum(before * is_label, axis=0, keepdims=True)
    slot = lax.broadcasted_iota(jnp.int32, (slots, count), 0).astype(F32)
    return jnp.where(slot == rank, 1.0, 0.0).astype(BF16)


def cycle_kernel(
    amp, itg, vir, occ, own, mirrored, slot_out,
    amp_own, int_own, amp_diag, int_diag, v_send, v_recv, part, part_recv, mid,
    v_ss, v_rs, col_ss, col_rs, row_ss, row_rs, part_ss, part_rs, hop_ss, hop_rs, end_ss, end_rs,
):
    slots = SLOTS
    half = amp.shape[3]
    I, J, h = lax.axis_index("row"), lax.axis_index("col"), lax.axis_index("vir")
    other = 1 - h
    diagonal = I == J
    partner = (I, J, other)

    apart = lax.rem(J - I + 16, 16)
    col_child = [lookup(apart, table, -1) for table in COL_TREE]
    col_parent = lookup(apart, {b: a for table in COL_TREE for a, b in table.items()}, 0)

    def along_col(offset):
        return (I, lax.rem(I + offset + 16, 16), h)

    dy = lax.rem(I // 8 + J // 8, 2)
    dx = lax.rem(lax.rem(I // 2, 4) - lax.rem(J // 2, 4) + 4, 4)
    dc = lax.rem(I + J, 2)

    def at_plane(y, x, core):
        row = lax.rem(J // 8 + y, 2) * 8 + lax.rem(lax.rem(J // 2, 4) + x, 4) * 2 + lax.rem(J + core, 2)
        return (row, J, h)

    first = dc == 0
    row_child = [
        (first, at_plane(dy, dx, 1)),
        (jnp.logical_and(first, dx == 0), at_plane(dy, 3, 0)),
        (jnp.logical_and(first, dx <= 1), at_plane(dy, dx + 1, 0)),
        (jnp.logical_and(first, dx + dy == 0), at_plane(1, 0, 0)),
    ]
    parent_y = jnp.where(jnp.logical_and(first, dx == 0), 0, dy)
    parent_x = jnp.where(first, jnp.where(dx == 2, 1, 0), dx)
    row_parent = at_plane(parent_y, parent_x, 0)

    r, s = I // 2, J // 2
    mid_row = lax.rem(5 * r + s, 8) * 2 + lax.rem(I, 2)
    from_row = lax.rem(5 * (r - s + 8), 8) * 2 + lax.rem(I, 2)
    back_row = lax.rem(5 * s + r, 8) * 2 + lax.rem(J, 2)
    mid_self = mid_row == I
    from_self = from_row == I
    end_self = jnp.logical_and(from_row == J, I == J)
    end_at = (J, from_row, h)

    barrier = pltpu.get_barrier_semaphore()

    def greet(device):
        pl.semaphore_signal(barrier, inc=1, device_id=device, device_id_type=MESH)

    greet(partner)

    @pl.when(jnp.logical_not(diagonal))
    def _():
        greet(along_col(col_parent))
        greet(row_parent)

    for v in range(2):
        @pl.when(jnp.logical_not(jnp.logical_and(from_self, h == v)))
        def _():
            greet((from_row, J, v))

    back_self = jnp.logical_and(back_row == I, I == J)

    @pl.when(jnp.logical_not(back_self))
    def _():
        greet((back_row, I, h))

    labels = [vir[:, w * half:(w + 1) * half] for w in range(2)]
    labels_here = jnp.where(h == 0, labels[0], labels[1])
    slot_of = [slot_matrix(labels[w], slots) for w in range(2)]
    for w in range(2):
        slot_out[:, w * half:(w + 1) * half] = slot_of[w]
    slot_here = jnp.where(h == 0, slot_of[0].astype(F32), slot_of[1].astype(F32)).astype(BF16)
    column = column_of(vir[...])
    column_here = jnp.where(h == 0, column[:half], column[half:])
    all_row = vir[...]

    cross_amp = column ^ labels_here
    cross_int = column_here ^ all_row
    for i in range(2):
        for k in range(2):
            g = occ[2 * I + i] ^ occ[2 * J + k]
            kept = jnp.where(cross_amp == g, amp[i, k].astype(F32), 0.0).astype(BF16)
            packed = dot(slot_here, kept, 1, 1)
            flipped = [dot(slot_of[w], kept[w * half:(w + 1) * half], 1, 0) for w in range(2)]
            flipped_here = jnp.where(h == 0, flipped[0], flipped[1])
            v_send[i * 2 + k] = jnp.where(h == 0, flipped[1], flipped[0]).astype(BF16)
            for w in range(2):
                piece = 2.0 * packed[:, w * half:(w + 1) * half]
                amp_own[i * 2 + k, :, w * half:(w + 1) * half] = jnp.where(h == w, piece - flipped_here, piece).astype(BF16)
            kept_int = jnp.where(cross_int == g, itg[i, k].astype(F32), 0.0).astype(BF16)
            int_own[k * 2 + i] = dot(slot_here, kept_int, 1, 0).astype(BF16)

    expected = jnp.int32(1)
    for child in col_child:
        expected += jnp.where(child >= 0, 1, 0)
    for there, _ in row_child:
        expected += jnp.where(there, 1, 0)
    expected += jnp.where(mid_self, 1, 2)
    expected += jnp.where(end_self, 0, 1)
    pl.semaphore_wait(barrier, expected)

    def v_copy(q):
        return remote(v_send.at[q], v_recv.at[q], v_ss.at[q], v_rs.at[q], partner)

    def col_copy(q, n):
        return remote(amp_diag.at[q], amp_diag.at[q], col_ss.at[n, q], col_rs.at[q], along_col(col_child[n]))

    def row_copy(q, n):
        return remote(int_diag.at[q], int_diag.at[q], row_ss.at[n, q], row_rs.at[q], row_child[n][1])

    def part_copy(q):
        return remote(part.at[other, q], part_recv.at[q], part_ss.at[q], part_rs.at[q], partner)

    def hop_copy(q, v, slot):
        return remote(own.at[v, q], mid.at[slot, q], hop_ss.at[v, q], hop_rs.at[slot, q], (mid_row, J, v))

    def end_copy(q, v):
        return remote(mid.at[v, q], mirrored.at[v, q], end_ss.at[v, q], end_rs.at[v, q], end_at)

    for q in range(4):
        v_copy(q).start()

    @pl.when(diagonal)
    def _():
        int_diag[...] = int_own[...]

    def row_forward(q):
        for n, (there, _) in reversed(list(enumerate(row_child))):
            @pl.when(there)
            def _():
                row_copy(q, n).start()

    def col_forward(q):
        for n, child in enumerate(col_child):
            @pl.when(child >= 0)
            def _():
                col_copy(q, n).start()

    @pl.when(diagonal)
    def _():
        for q in range(4):
            row_forward(q)

    rest = pl.ds(pl.multiple_of(other * half, half), half)
    for q in range(4):
        v_copy(q).wait_recv()
        amp_own[q, :, rest] = (amp_own[q, :, rest].astype(F32) - v_recv[q].astype(F32)).astype(BF16)

        @pl.when(diagonal)
        def _():
            amp_diag[q] = amp_own[q]
            amp_own[q] = jnp.zeros(amp_own.shape[1:], BF16)
            col_forward(q)

    @pl.when(jnp.logical_not(diagonal))
    def _():
        for q in range(4):
            row_copy(q, 0).wait_recv()
            row_forward(q)
        for q in range(4):
            col_copy(q, 0).wait_recv()
            col_forward(q)

    def both(ref, n):
        return ref[2 * n:2 * n + 2].reshape(2 * slots, 2 * half)

    cross = column ^ all_row
    for i in range(2):
        for j in range(2):
            g = occ[2 * I + i] ^ occ[2 * J + j]
            total = dot(both(int_own, j), both(amp_diag, i), 0, 0) + dot(both(int_diag, j), both(amp_own, i), 0, 0)
            total = jnp.where(cross == g, total, 0.0).astype(BF16)
            q = i * 2 + j
            for w in range(2):
                part[w, q] = dot(slot_of[w], total[w * half:(w + 1) * half], 1, 0).astype(BF16)
            part_copy(q).start()

    for q in range(4):
        part_copy(q).wait_recv()
        cycle = (part[h, q].astype(F32) + part_recv[q].astype(F32)).astype(BF16)
        for v in range(2):
            own[v, q] = cycle[:, v * half:(v + 1) * half]
            to_self = jnp.logical_and(mid_self, h == v)

            @pl.when(to_self)
            def _():
                mid[v, q] = own[v, q]

            @pl.when(jnp.logical_not(to_self))
            def _():
                hop_copy(q, v, h).start()

    for q in range(4):
        for v in range(2):
            @pl.when(jnp.logical_not(jnp.logical_and(from_self, h == v)))
            def _():
                hop_copy(q, v, v).wait_recv()

            @pl.when(end_self)
            def _():
                mirrored[v, q] = mid[v, q]

            @pl.when(jnp.logical_not(end_self))
            def _():
                end_copy(q, v).start()

    for q in range(4):
        for v in range(2):
            @pl.when(jnp.logical_not(back_self))
            def _():
                end_copy(q, v).wait_recv()

    for q in range(4):
        v_copy(q).wait_send()
        part_copy(q).wait_send()
        for n, child in enumerate(col_child):
            @pl.when(child >= 0)
            def _():
                col_copy(q, n).wait_send()
        for n, (there, _) in enumerate(row_child):
            @pl.when(there)
            def _():
                row_copy(q, n).wait_send()
        for v in range(2):
            @pl.when(jnp.logical_not(jnp.logical_and(mid_self, h == v)))
            def _():
                hop_copy(q, v, v).wait_send()

            @pl.when(jnp.logical_not(end_self))
            def _():
                end_copy(q, v).wait_send()


def unpack_kernel(own, mirrored, slot_of, vir, occ, out):
    half = out.shape[3]
    I, J, h = lax.axis_index("row"), lax.axis_index("col"), lax.axis_index("vir")
    i, j = pl.program_id(0), pl.program_id(1)
    g = occ[2 * I + i] ^ occ[2 * J + j]
    here = pl.ds(pl.multiple_of(h * half, half), half)
    cross = column_of(vir[...]) ^ vir[:, here]
    for v in range(2):
        rows = slice(v * half, (v + 1) * half)
        left = jnp.concatenate([own[v, i * 2 + j], slot_of[:, rows]], axis=0)
        right = jnp.concatenate([slot_of[:, here], mirrored[v, j * 2 + i]], axis=0)
        out[0, 0, rows] = jnp.where(cross[rows] == g, dot(left, right, 0, 0), 0.0)


def packed_plan(amplitudes, integrals, occ_irrep, vir_irrep):
    half = amplitudes.shape[3]
    full = 2 * half
    vmem = pl.BlockSpec(memory_space=pltpu.VMEM)
    smem = pl.BlockSpec(memory_space=pltpu.SMEM)
    vir = vir_irrep.reshape(1, full)
    tile = pltpu.VMEM((4, SLOTS, full), BF16)
    dma = pltpu.SemaphoreType.DMA
    halves = jax.ShapeDtypeStruct((2, 4, SLOTS, half), BF16)
    own, mirrored, slot_of = pl.pallas_call(
        cycle_kernel,
        out_shape=[halves, halves, jax.ShapeDtypeStruct((SLOTS, full), BF16)],
        in_specs=[vmem, vmem, vmem, smem],
        out_specs=[vmem, vmem, vmem],
        scratch_shapes=[
            tile, tile, tile, tile,
            pltpu.VMEM((4, SLOTS, half), BF16), pltpu.VMEM((4, SLOTS, half), BF16),
            pltpu.VMEM((2, 4, SLOTS, full), BF16), tile, pltpu.VMEM((2, 4, SLOTS, half), BF16),
            dma((4,)), dma((4,)), dma((4, 4)), dma((4,)), dma((4, 4)), dma((4,)), dma((4,)), dma((4,)),
            dma((2, 4)), dma((2, 4)), dma((2, 4)), dma((2, 4)),
        ],
        compiler_params=pltpu.CompilerParams(
            collective_id=0, has_side_effects=True, vmem_limit_bytes=32 * 2**20
        ),
    )(amplitudes, integrals, vir, occ_irrep)
    return pl.pallas_call(
        unpack_kernel,
        grid=(2, 2),
        out_shape=jax.ShapeDtypeStruct((2, 2, full, half), F32),
        in_specs=[vmem, vmem, vmem, vmem, smem],
        out_specs=pl.BlockSpec((1, 1, full, half), lambda i, j: (i, j, 0, 0)),
        compiler_params=pltpu.CompilerParams(vmem_limit_bytes=32 * 2**20),
    )(own, mirrored, slot_of, vir, occ_irrep)


def from_partner(value, axis, apart):
    mask = 2**apart
    pairs = [(source, source ^ mask) for source in range(lax.axis_size(axis))]
    return lax.ppermute(value, axis, pairs)


def broadcast(value, axis, source):
    kept = jnp.where(lax.axis_index(axis) == source, value, 0).astype(value.dtype)
    return lax.psum(kept, axis)


def symmetry_mask(left, right, first, second):
    return (
        left[:, None, None, None]
        ^ right[None, :, None, None]
        ^ first[None, None, :, None]
        ^ second[None, None, None, :]
        == 0
    )


def contract(amplitude_tile, integral_tile):
    return jnp.einsum(
        "ikac,kjcb->ijab", amplitude_tile, integral_tile, preferred_element_type=jnp.float32
    )


def mirror(values, row_index, col_index):
    levels = lax.axis_size("row").bit_length() - 1
    for section_bit in range(levels):
        across = from_partner(values, "row", section_bit)
        across = from_partner(across, "col", section_bit)
        differ = row_index >> section_bit & 1 != col_index >> section_bit & 1
        values = jnp.where(differ, across, values)
    return values


def whole_plan(amplitudes, integrals, occ_irrep, vir_irrep):
    block_size = amplitudes.shape[0]
    virtual_count = amplitudes.shape[2]
    half_count = amplitudes.shape[3]
    row_index = lax.axis_index("row")
    col_index = lax.axis_index("col")
    half_index = lax.axis_index("vir")
    occ_row = lax.dynamic_slice_in_dim(occ_irrep, row_index * block_size, block_size)
    occ_col = lax.dynamic_slice_in_dim(occ_irrep, col_index * block_size, block_size)
    vir_half = lax.dynamic_slice_in_dim(vir_irrep, half_index * half_count, half_count)
    amp_masked = jnp.where(
        symmetry_mask(occ_row, occ_col, vir_irrep, vir_half), amplitudes, jnp.zeros_like(amplitudes)
    )
    int_masked = jnp.where(
        symmetry_mask(occ_row, occ_col, vir_half, vir_irrep), integrals, jnp.zeros_like(integrals)
    )
    flipped = lax.all_to_all(amp_masked, "vir", split_axis=2, concat_axis=3, tiled=True)
    combined = (
        2.0 * amp_masked.astype(jnp.float32)
        - jnp.transpose(flipped, (0, 1, 3, 2)).astype(jnp.float32)
    ).astype(jnp.bfloat16)
    off_diagonal = row_index != col_index
    empty_shape = (block_size, block_size, virtual_count, virtual_count)
    amp_row_diag = broadcast(combined, "col", row_index)
    int_col_diag = broadcast(int_masked, "row", col_index)
    own_term = contract(amp_row_diag, int_masked) + lax.cond(
        off_diagonal,
        lambda: contract(combined, int_col_diag),
        lambda: jnp.zeros(empty_shape, jnp.float32),
    )
    own_sum = lax.psum_scatter(
        own_term.astype(jnp.bfloat16), "vir", scatter_dimension=3, tiled=True
    )
    facing = mirror(own_sum, row_index, col_index)
    paired = lax.all_to_all(facing, "vir", split_axis=2, concat_axis=3, tiled=True)
    return own_sum.astype(jnp.float32) + jnp.transpose(paired, (1, 0, 3, 2)).astype(jnp.float32)


def on_device(amplitudes, integrals, occ_irrep, vir_irrep):
    halves = vir_irrep.reshape(2, -1, 1) == jnp.arange(LABELS, dtype=jnp.int32)
    most = jnp.max(jnp.sum(halves.astype(jnp.int32), axis=1))
    return lax.cond(most <= SLOTS, packed_plan, whole_plan, amplitudes, integrals, occ_irrep, vir_irrep)


def solution(mesh):
    return jax.shard_map(
        on_device,
        mesh=mesh,
        in_specs=(P("row", "col", None, "vir"), P("row", "col", "vir", None), P(), P()),
        out_specs=P("row", "col", None, "vir"),
        check_vma=False,
    )
```

```python
import functools

import jax
import jax.numpy as jnp
from jax import lax
from jax.experimental import pallas as pl
from jax.experimental.pallas import tpu as pltpu
from jax.sharding import PartitionSpec as P

MESH = pl.DeviceIdType.MESH
LABELS = 8
SLOTS = 48
F32 = jnp.float32
BF16 = jnp.bfloat16

COL_TREE = (
    {0: 4, 4: 8, 8: 7, 12: 11, 11: 10, 5: 6, 3: 2, 15: 14},
    {0: 12, 4: 5, 8: 9, 12: 13},
    {0: 1, 4: 3},
    {0: 15},
)


def lookup(key, table, default):
    found = jnp.int32(default)
    for at, value in table.items():
        found = jnp.where(key == at, jnp.int32(value), found)
    return found


def dot(left, right, left_dim, right_dim):
    return lax.dot_general(left, right, (((left_dim,), (right_dim,)), ((), ())), preferred_element_type=F32)


def remote(src, dst, send_sem, recv_sem, device):
    return pltpu.make_async_remote_copy(
        src_ref=src, dst_ref=dst, send_sem=send_sem, recv_sem=recv_sem, device_id=device, device_id_type=MESH
    )


def column_of(row_labels):
    return jnp.broadcast_to(row_labels, (128, row_labels.shape[1])).T[:, :1]


def slot_matrix(labels, slots):
    count = labels.shape[1]
    is_label = (lax.broadcasted_iota(jnp.int32, (LABELS, count), 0) == labels).astype(F32)
    earlier = (
        lax.broadcasted_iota(jnp.int32, (count, count), 0) < lax.broadcasted_iota(jnp.int32, (count, count), 1)
    ).astype(F32)
    before = dot(is_label.astype(BF16), earlier.astype(BF16), 1, 0)
    rank = jnp.sum(before * is_label, axis=0, keepdims=True)
    slot = lax.broadcasted_iota(jnp.int32, (slots, count), 0).astype(F32)
    return jnp.where(slot == rank, 1.0, 0.0).astype(BF16)


def cycle_kernel(
    amp_hbm, int_hbm, vir, occ, own, mirrored, slot_out,
    amp, itg, load_sem, amp_own, int_own, amp_diag, int_diag, v_send, v_recv, part, part_recv, mid,
    v_ss, v_rs, col_ss, col_rs, row_ss, row_rs, part_ss, part_rs, hop_ss, hop_rs, end_ss, end_rs,
):
    slots = SLOTS
    half = amp.shape[3]
    I, J, h = lax.axis_index("row"), lax.axis_index("col"), lax.axis_index("vir")
    other = 1 - h
    loads = [pltpu.make_async_copy(amp_hbm, amp, load_sem.at[0]), pltpu.make_async_copy(int_hbm, itg, load_sem.at[1])]
    for load in loads:
        load.start()
    diagonal = I == J
    partner = (I, J, other)

    apart = lax.rem(J - I + 16, 16)
    col_child = [lookup(apart, table, -1) for table in COL_TREE]
    col_parent = lookup(apart, {b: a for table in COL_TREE for a, b in table.items()}, 0)

    def along_col(offset):
        return (I, lax.rem(I + offset + 16, 16), h)

    dy = lax.rem(I // 8 + J // 8, 2)
    dx = lax.rem(lax.rem(I // 2, 4) - lax.rem(J // 2, 4) + 4, 4)
    dc = lax.rem(I + J, 2)

    def at_plane(y, x, core):
        row = lax.rem(J // 8 + y, 2) * 8 + lax.rem(lax.rem(J // 2, 4) + x, 4) * 2 + lax.rem(J + core, 2)
        return (row, J, h)

    first = dc == 0
    row_child = [
        (first, at_plane(dy, dx, 1)),
        (jnp.logical_and(first, dx == 0), at_plane(dy, 3, 0)),
        (jnp.logical_and(first, dx <= 1), at_plane(dy, dx + 1, 0)),
        (jnp.logical_and(first, dx + dy == 0), at_plane(1, 0, 0)),
    ]
    parent_y = jnp.where(jnp.logical_and(first, dx == 0), 0, dy)
    parent_x = jnp.where(first, jnp.where(dx == 2, 1, 0), dx)
    row_parent = at_plane(parent_y, parent_x, 0)

    r, s = I // 2, J // 2
    mid_row = lax.rem(5 * r + s, 8) * 2 + lax.rem(I, 2)
    from_row = lax.rem(5 * (r - s + 8), 8) * 2 + lax.rem(I, 2)
    back_row = lax.rem(5 * s + r, 8) * 2 + lax.rem(J, 2)
    mid_self = mid_row == I
    from_self = from_row == I
    end_self = jnp.logical_and(from_row == J, I == J)
    end_at = (J, from_row, h)

    barrier = pltpu.get_barrier_semaphore()

    def greet(device):
        pl.semaphore_signal(barrier, inc=1, device_id=device, device_id_type=MESH)

    greet(partner)

    @pl.when(jnp.logical_not(diagonal))
    def _():
        greet(along_col(col_parent))
        greet(row_parent)

    for v in range(2):
        @pl.when(jnp.logical_not(jnp.logical_and(from_self, h == v)))
        def _():
            greet((from_row, J, v))

    back_self = jnp.logical_and(back_row == I, I == J)

    @pl.when(jnp.logical_not(back_self))
    def _():
        greet((back_row, I, h))

    labels = [vir[:, w * half:(w + 1) * half] for w in range(2)]
    labels_here = jnp.where(h == 0, labels[0], labels[1])
    slot_of = [slot_matrix(labels[w], slots) for w in range(2)]
    for w in range(2):
        slot_out[:, w * half:(w + 1) * half] = slot_of[w]
    slot_here = jnp.where(h == 0, slot_of[0].astype(F32), slot_of[1].astype(F32)).astype(BF16)
    column = column_of(vir[...])
    column_here = jnp.where(h == 0, column[:half], column[half:])
    all_row = vir[...]

    for load in loads:
        load.wait()
    cross_amp = column ^ labels_here
    cross_int = column_here ^ all_row
    for i in range(2):
        for k in range(2):
            g = occ[2 * I + i] ^ occ[2 * J + k]
            kept = jnp.where(cross_amp == g, amp[i, k].astype(F32), 0.0).astype(BF16)
            packed = dot(slot_here, kept, 1, 1)
            flipped = [dot(slot_of[w], kept[w * half:(w + 1) * half], 1, 0) for w in range(2)]
            flipped_here = jnp.where(h == 0, flipped[0], flipped[1])
            v_send[i * 2 + k] = jnp.where(h == 0, flipped[1], flipped[0]).astype(BF16)
            for w in range(2):
                piece = 2.0 * packed[:, w * half:(w + 1) * half]
                amp_own[i * 2 + k, :, w * half:(w + 1) * half] = jnp.where(h == w, piece - flipped_here, piece).astype(BF16)
            kept_int = jnp.where(cross_int == g, itg[i, k].astype(F32), 0.0).astype(BF16)
            int_own[k * 2 + i] = dot(slot_here, kept_int, 1, 0).astype(BF16)

    expected = jnp.int32(1)
    for child in col_child:
        expected += jnp.where(child >= 0, 1, 0)
    for there, _ in row_child:
        expected += jnp.where(there, 1, 0)
    expected += jnp.where(mid_self, 1, 2)
    expected += jnp.where(end_self, 0, 1)
    pl.semaphore_wait(barrier, expected)

    def v_copy(q):
        return remote(v_send.at[q], v_recv.at[q], v_ss.at[q], v_rs.at[q], partner)

    def col_copy(q, n):
        return remote(amp_diag.at[q], amp_diag.at[q], col_ss.at[n, q], col_rs.at[q], along_col(col_child[n]))

    def row_copy(q, n):
        return remote(int_diag.at[q], int_diag.at[q], row_ss.at[n, q], row_rs.at[q], row_child[n][1])

    def part_copy(q):
        return remote(part.at[other, q], part_recv.at[q], part_ss.at[q], part_rs.at[q], partner)

    def hop_copy(q, v, slot):
        return remote(own.at[v, q], mid.at[slot, q], hop_ss.at[v, q], hop_rs.at[slot, q], (mid_row, J, v))

    def end_copy(q, v):
        return remote(mid.at[v, q], mirrored.at[v, q], end_ss.at[v, q], end_rs.at[v, q], end_at)

    for q in range(4):
        v_copy(q).start()

    @pl.when(diagonal)
    def _():
        int_diag[...] = int_own[...]

    def row_forward(q):
        for n, (there, _) in reversed(list(enumerate(row_child))):
            @pl.when(there)
            def _():
                row_copy(q, n).start()

    def col_forward(q):
        for n, child in enumerate(col_child):
            @pl.when(child >= 0)
            def _():
                col_copy(q, n).start()

    @pl.when(diagonal)
    def _():
        for q in range(4):
            row_forward(q)

    rest = pl.ds(pl.multiple_of(other * half, half), half)
    for q in range(4):
        v_copy(q).wait_recv()
        amp_own[q, :, rest] = (amp_own[q, :, rest].astype(F32) - v_recv[q].astype(F32)).astype(BF16)

        @pl.when(diagonal)
        def _():
            amp_diag[q] = amp_own[q]
            amp_own[q] = jnp.zeros(amp_own.shape[1:], BF16)
            col_forward(q)

    @pl.when(jnp.logical_not(diagonal))
    def _():
        for q in range(4):
            row_copy(q, 0).wait_recv()
            row_forward(q)
        for q in range(4):
            col_copy(q, 0).wait_recv()
            col_forward(q)

    def both(ref, n):
        return ref[2 * n:2 * n + 2].reshape(2 * slots, 2 * half)

    cross = column ^ all_row
    for i in range(2):
        for j in range(2):
            g = occ[2 * I + i] ^ occ[2 * J + j]
            total = dot(both(int_own, j), both(amp_diag, i), 0, 0) + dot(both(int_diag, j), both(amp_own, i), 0, 0)
            total = jnp.where(cross == g, total, 0.0).astype(BF16)
            q = i * 2 + j
            for w in range(2):
                part[w, q] = dot(slot_of[w], total[w * half:(w + 1) * half], 1, 0).astype(BF16)
            part_copy(q).start()

    for q in range(4):
        part_copy(q).wait_recv()
        cycle = (part[h, q].astype(F32) + part_recv[q].astype(F32)).astype(BF16)
        for v in range(2):
            own[v, q] = cycle[:, v * half:(v + 1) * half]
            to_self = jnp.logical_and(mid_self, h == v)

            @pl.when(to_self)
            def _():
                mid[v, q] = own[v, q]

            @pl.when(jnp.logical_not(to_self))
            def _():
                hop_copy(q, v, h).start()

    for q in range(4):
        for v in range(2):
            @pl.when(jnp.logical_not(jnp.logical_and(from_self, h == v)))
            def _():
                hop_copy(q, v, v).wait_recv()

            @pl.when(end_self)
            def _():
                mirrored[v, q] = mid[v, q]

            @pl.when(jnp.logical_not(end_self))
            def _():
                end_copy(q, v).start()

    for q in range(4):
        for v in range(2):
            @pl.when(jnp.logical_not(back_self))
            def _():
                end_copy(q, v).wait_recv()

    for q in range(4):
        v_copy(q).wait_send()
        part_copy(q).wait_send()
        for n, child in enumerate(col_child):
            @pl.when(child >= 0)
            def _():
                col_copy(q, n).wait_send()
        for n, (there, _) in enumerate(row_child):
            @pl.when(there)
            def _():
                row_copy(q, n).wait_send()
        for v in range(2):
            @pl.when(jnp.logical_not(jnp.logical_and(mid_self, h == v)))
            def _():
                hop_copy(q, v, v).wait_send()

            @pl.when(jnp.logical_not(end_self))
            def _():
                end_copy(q, v).wait_send()


def unpack_kernel(own, mirrored, slot_of, vir, occ, out):
    half = out.shape[3]
    I, J, h = lax.axis_index("row"), lax.axis_index("col"), lax.axis_index("vir")
    i, j = pl.program_id(0), pl.program_id(1)
    g = occ[2 * I + i] ^ occ[2 * J + j]
    here = pl.ds(pl.multiple_of(h * half, half), half)
    cross = column_of(vir[...]) ^ vir[:, here]
    for v in range(2):
        rows = slice(v * half, (v + 1) * half)
        left = jnp.concatenate([own[v, i * 2 + j], slot_of[:, rows]], axis=0)
        right = jnp.concatenate([slot_of[:, here], mirrored[v, j * 2 + i]], axis=0)
        out[0, 0, rows] = jnp.where(cross[rows] == g, dot(left, right, 0, 0), 0.0)


def packed_plan(amplitudes, integrals, occ_irrep, vir_irrep):
    half = amplitudes.shape[3]
    full = 2 * half
    vmem = pl.BlockSpec(memory_space=pltpu.VMEM)
    smem = pl.BlockSpec(memory_space=pltpu.SMEM)
    vir = vir_irrep.reshape(1, full)
    tile = pltpu.VMEM((4, SLOTS, full), BF16)
    dma = pltpu.SemaphoreType.DMA
    halves = jax.ShapeDtypeStruct((2, 4, SLOTS, half), BF16)
    own, mirrored, slot_of = pl.pallas_call(
        cycle_kernel,
        out_shape=[halves, halves, jax.ShapeDtypeStruct((SLOTS, full), BF16)],
        in_specs=[pl.BlockSpec(memory_space=pl.ANY)] * 2 + [vmem, smem],
        out_specs=[vmem, vmem, vmem],
        scratch_shapes=[
            pltpu.VMEM(amplitudes.shape, BF16), pltpu.VMEM(integrals.shape, BF16), dma((2,)),
            tile, tile, tile, tile,
            pltpu.VMEM((4, SLOTS, half), BF16), pltpu.VMEM((4, SLOTS, half), BF16),
            pltpu.VMEM((2, 4, SLOTS, full), BF16), tile, pltpu.VMEM((2, 4, SLOTS, half), BF16),
            dma((4,)), dma((4,)), dma((4, 4)), dma((4,)), dma((4, 4)), dma((4,)), dma((4,)), dma((4,)),
            dma((2, 4)), dma((2, 4)), dma((2, 4)), dma((2, 4)),
        ],
        compiler_params=pltpu.CompilerParams(
            collective_id=0, has_side_effects=True, vmem_limit_bytes=32 * 2**20
        ),
    )(amplitudes, integrals, vir, occ_irrep)
    return pl.pallas_call(
        unpack_kernel,
        grid=(2, 2),
        out_shape=jax.ShapeDtypeStruct((2, 2, full, half), F32),
        in_specs=[vmem, vmem, vmem, vmem, smem],
        out_specs=pl.BlockSpec((1, 1, full, half), lambda i, j: (i, j, 0, 0)),
        compiler_params=pltpu.CompilerParams(vmem_limit_bytes=32 * 2**20),
    )(own, mirrored, slot_of, vir, occ_irrep)


def from_diagonal(value, row_index, col_index, along):
    size = lax.axis_size("col")
    apart = (col_index - row_index if along == "col" else row_index - col_index) % size
    reach = 1
    while reach < size:
        pairs = []
        for near in range(size):
            for step in range(reach):
                source, target = (near + step) % size, (near + step + reach) % size
                if along == "col":
                    pairs.append((near * size + source, near * size + target))
                else:
                    pairs.append((source * size + near, target * size + near))
        moved = lax.ppermute(value, ("row", "col"), pairs)
        value = jnp.where(jnp.logical_and(apart >= reach, apart < 2 * reach), moved, value)
        reach *= 2
    return value


def from_other_half(value):
    return lax.ppermute(value, "vir", [(0, 1), (1, 0)])


def symmetry_mask(left, right, first, second):
    return (
        left[:, None, None, None]
        ^ right[None, :, None, None]
        ^ first[None, None, :, None]
        ^ second[None, None, None, :]
        == 0
    )


def contract(amplitude_tile, integral_tile):
    return jnp.einsum(
        "ikac,kjcb->ijab", amplitude_tile, integral_tile, preferred_element_type=jnp.float32
    )


def from_mirror(value):
    size = lax.axis_size("col")
    pairs = [(i * size + j, j * size + i) for i in range(size) for j in range(size)]
    return lax.ppermute(value, ("row", "col"), pairs)


def whole_plan(amplitudes, integrals, occ_irrep, vir_irrep):
    block_size = amplitudes.shape[0]
    virtual_count = amplitudes.shape[2]
    half_count = amplitudes.shape[3]
    row_index = lax.axis_index("row")
    col_index = lax.axis_index("col")
    half_index = lax.axis_index("vir")
    occ_row = lax.dynamic_slice_in_dim(occ_irrep, row_index * block_size, block_size)
    occ_col = lax.dynamic_slice_in_dim(occ_irrep, col_index * block_size, block_size)
    vir_half = lax.dynamic_slice_in_dim(vir_irrep, half_index * half_count, half_count)
    amp_masked = jnp.where(
        symmetry_mask(occ_row, occ_col, vir_irrep, vir_half), amplitudes, jnp.zeros_like(amplitudes)
    )
    int_masked = jnp.where(
        symmetry_mask(occ_row, occ_col, vir_half, vir_irrep), integrals, jnp.zeros_like(integrals)
    )
    flipped = lax.all_to_all(amp_masked, "vir", split_axis=2, concat_axis=3, tiled=True)
    combined = (
        2.0 * amp_masked.astype(jnp.float32)
        - jnp.transpose(flipped, (0, 1, 3, 2)).astype(jnp.float32)
    ).astype(jnp.bfloat16)
    off_diagonal = row_index != col_index
    empty_shape = (block_size, block_size, virtual_count, virtual_count)
    amp_row_diag = from_diagonal(combined, row_index, col_index, "col")
    int_col_diag = from_diagonal(int_masked, row_index, col_index, "row")
    own_term = contract(amp_row_diag, int_masked) + lax.cond(
        off_diagonal,
        lambda: contract(combined, int_col_diag),
        lambda: jnp.zeros(empty_shape, jnp.float32),
    )
    rounded = own_term.astype(jnp.bfloat16)
    kept = lax.dynamic_slice_in_dim(rounded, half_index * half_count, half_count, 3)
    moved = from_other_half(lax.dynamic_slice_in_dim(rounded, (1 - half_index) * half_count, half_count, 3))
    own_sum = (kept.astype(jnp.float32) + moved.astype(jnp.float32)).astype(jnp.bfloat16)
    facing = from_mirror(own_sum)
    paired = lax.all_to_all(facing, "vir", split_axis=2, concat_axis=3, tiled=True)
    return own_sum.astype(jnp.float32) + jnp.transpose(paired, (1, 0, 3, 2)).astype(jnp.float32)


def on_device(amplitudes, integrals, occ_irrep, vir_irrep):
    halves = vir_irrep.reshape(2, -1, 1) == jnp.arange(LABELS, dtype=jnp.int32)
    most = jnp.max(jnp.sum(halves.astype(jnp.int32), axis=1))
    return lax.cond(most <= SLOTS, packed_plan, whole_plan, amplitudes, integrals, occ_irrep, vir_irrep)


def solution(mesh):
    return jax.shard_map(
        on_device,
        mesh=mesh,
        in_specs=(P("row", "col", None, "vir"), P("row", "col", "vir", None), P(), P()),
        out_specs=P("row", "col", None, "vir"),
        check_vma=False,
    )
```

```python
import functools

import jax
import jax.numpy as jnp
from jax import lax
from jax.experimental import pallas as pl
from jax.experimental.pallas import tpu as pltpu
from jax.sharding import PartitionSpec as P

MESH = pl.DeviceIdType.MESH
LABELS = 8
SLOTS = 48
F32 = jnp.float32
BF16 = jnp.bfloat16

COL_TREE = (
    {0: 8, 8: 7, 4: 5, 5: 6, 12: 11, 11: 10, 1: 2, 15: 14},
    {0: 4, 8: 9, 4: 3, 12: 13},
    {0: 12},
    {0: 1},
    {0: 15},
)


def lookup(key, table, default):
    found = jnp.int32(default)
    for at, value in table.items():
        found = jnp.where(key == at, jnp.int32(value), found)
    return found


def dot(left, right, left_dim, right_dim):
    return lax.dot_general(left, right, (((left_dim,), (right_dim,)), ((), ())), preferred_element_type=F32)


def remote(src, dst, send_sem, recv_sem, device):
    return pltpu.make_async_remote_copy(
        src_ref=src, dst_ref=dst, send_sem=send_sem, recv_sem=recv_sem, device_id=device, device_id_type=MESH
    )


def column_of(row_labels):
    return jnp.broadcast_to(row_labels, (128, row_labels.shape[1])).T[:, :1]


def slot_matrix(labels, slots):
    count = labels.shape[1]
    is_label = (lax.broadcasted_iota(jnp.int32, (LABELS, count), 0) == labels).astype(F32)
    earlier = (
        lax.broadcasted_iota(jnp.int32, (count, count), 0) < lax.broadcasted_iota(jnp.int32, (count, count), 1)
    ).astype(F32)
    before = dot(is_label.astype(BF16), earlier.astype(BF16), 1, 0)
    rank = jnp.sum(before * is_label, axis=0, keepdims=True)
    slot = lax.broadcasted_iota(jnp.int32, (slots, count), 0).astype(F32)
    return jnp.where(slot == rank, 1.0, 0.0).astype(BF16), jnp.max(rank)


def cycle_kernel(
    amp_hbm, int_hbm, vir, occ, own, mirrored, slot_out, most_out,
    amp, itg, load_sem, amp_own, int_own, amp_diag, int_diag, v_send, v_recv, part, part_recv, mid,
    v_ss, v_rs, col_ss, col_rs, row_ss, row_rs, part_ss, part_rs, hop_ss, hop_rs, end_ss, end_rs,
):
    slots = SLOTS
    half = amp.shape[3]
    I, J, h = lax.axis_index("row"), lax.axis_index("col"), lax.axis_index("vir")
    other = 1 - h
    loads = [pltpu.make_async_copy(amp_hbm, amp, load_sem.at[0]), pltpu.make_async_copy(int_hbm, itg, load_sem.at[1])]
    for load in loads:
        load.start()
    diagonal = I == J
    partner = (I, J, other)

    apart = lax.rem(J - I + 16, 16)
    col_child = [lookup(apart, table, -1) for table in COL_TREE]
    col_parent = lookup(apart, {b: a for table in COL_TREE for a, b in table.items()}, 0)

    def along_col(offset):
        return (I, lax.rem(I + offset + 16, 16), h)

    dy = lax.rem(I // 8 + J // 8, 2)
    dx = lax.rem(lax.rem(I // 2, 4) - lax.rem(J // 2, 4) + 4, 4)
    dc = lax.rem(I + J, 2)

    def at_plane(y, x, core):
        row = lax.rem(J // 8 + y, 2) * 8 + lax.rem(lax.rem(J // 2, 4) + x, 4) * 2 + lax.rem(J + core, 2)
        return (row, J, h)

    first = dc == 0
    row_child = [
        (first, at_plane(dy, dx, 1)),
        (jnp.logical_and(first, dx == 0), at_plane(dy, 2, 0)),
        (jnp.logical_and(first, dx == 0), at_plane(dy, 3, 0)),
        (jnp.logical_and(first, dx == 0), at_plane(dy, 1, 0)),
        (jnp.logical_and(first, dx + dy == 0), at_plane(1, 0, 0)),
    ]
    parent_y = jnp.where(jnp.logical_and(first, dx == 0), 0, dy)
    parent_x = jnp.where(first, 0, dx)
    row_parent = at_plane(parent_y, parent_x, 0)

    r, s = I // 2, J // 2
    mid_row = lax.rem(5 * r + s, 8) * 2 + lax.rem(I, 2)
    from_row = lax.rem(5 * (r - s + 8), 8) * 2 + lax.rem(I, 2)
    back_row = lax.rem(5 * s + r, 8) * 2 + lax.rem(J, 2)
    mid_self = mid_row == I
    from_self = from_row == I
    end_self = jnp.logical_and(from_row == J, I == J)
    end_at = (J, from_row, h)

    barrier = pltpu.get_barrier_semaphore()

    def greet(device):
        pl.semaphore_signal(barrier, inc=1, device_id=device, device_id_type=MESH)

    greet(partner)

    @pl.when(jnp.logical_not(diagonal))
    def _():
        greet(along_col(col_parent))
        greet(row_parent)

    for v in range(2):
        @pl.when(jnp.logical_not(jnp.logical_and(from_self, h == v)))
        def _():
            greet((from_row, J, v))

    back_self = jnp.logical_and(back_row == I, I == J)

    @pl.when(jnp.logical_not(back_self))
    def _():
        greet((back_row, I, h))

    labels = [vir[:, w * half:(w + 1) * half] for w in range(2)]
    labels_here = jnp.where(h == 0, labels[0], labels[1])
    (slot_low, most_low), (slot_high, most_high) = [slot_matrix(labels[w], slots) for w in range(2)]
    slot_of = [slot_low, slot_high]
    most_out[...] = jnp.full((1, 1), jnp.maximum(most_low, most_high), F32)
    for w in range(2):
        slot_out[:, w * half:(w + 1) * half] = slot_of[w]
    slot_here = jnp.where(h == 0, slot_of[0].astype(F32), slot_of[1].astype(F32)).astype(BF16)
    column = column_of(vir[...])
    column_here = jnp.where(h == 0, column[:half], column[half:])
    all_row = vir[...]

    for load in loads:
        load.wait()
    cross_amp = column ^ labels_here
    cross_int = column_here ^ all_row
    for i in range(2):
        for k in range(2):
            g = occ[2 * I + i] ^ occ[2 * J + k]
            kept = jnp.where(cross_amp == g, amp[i, k].astype(F32), 0.0).astype(BF16)
            packed = dot(slot_here, kept, 1, 1)
            flipped = [dot(slot_of[w], kept[w * half:(w + 1) * half], 1, 0) for w in range(2)]
            flipped_here = jnp.where(h == 0, flipped[0], flipped[1])
            v_send[i * 2 + k] = jnp.where(h == 0, flipped[1], flipped[0]).astype(BF16)
            for w in range(2):
                piece = 2.0 * packed[:, w * half:(w + 1) * half]
                amp_own[i * 2 + k, :, w * half:(w + 1) * half] = jnp.where(h == w, piece - flipped_here, piece).astype(BF16)
            kept_int = jnp.where(cross_int == g, itg[i, k].astype(F32), 0.0).astype(BF16)
            int_own[k * 2 + i] = dot(slot_here, kept_int, 1, 0).astype(BF16)

    expected = jnp.int32(1)
    for child in col_child:
        expected += jnp.where(child >= 0, 1, 0)
    for there, _ in row_child:
        expected += jnp.where(there, 1, 0)
    expected += jnp.where(mid_self, 1, 2)
    expected += jnp.where(end_self, 0, 1)
    pl.semaphore_wait(barrier, expected)

    def v_copy(q):
        return remote(v_send.at[q], v_recv.at[q], v_ss.at[q], v_rs.at[q], partner)

    def col_copy(q, n):
        return remote(amp_diag.at[q], amp_diag.at[q], col_ss.at[n, q], col_rs.at[q], along_col(col_child[n]))

    def row_copy(q, n):
        return remote(int_diag.at[q], int_diag.at[q], row_ss.at[n, q], row_rs.at[q], row_child[n][1])

    def part_copy(q):
        return remote(part.at[other, q], part_recv.at[q], part_ss.at[q], part_rs.at[q], partner)

    def hop_copy(q, v, slot):
        return remote(own.at[v, q], mid.at[slot, q], hop_ss.at[v, q], hop_rs.at[slot, q], (mid_row, J, v))

    def end_copy(q, v):
        return remote(mid.at[v, q], mirrored.at[v, q], end_ss.at[v, q], end_rs.at[v, q], end_at)

    for q in range(4):
        v_copy(q).start()

    @pl.when(diagonal)
    def _():
        int_diag[...] = int_own[...]

    def row_forward(q):
        for n, (there, _) in reversed(list(enumerate(row_child))):
            @pl.when(there)
            def _():
                row_copy(q, n).start()

    def col_forward(q):
        for n, child in enumerate(col_child):
            @pl.when(child >= 0)
            def _():
                col_copy(q, n).start()

    @pl.when(diagonal)
    def _():
        for q in range(4):
            row_forward(q)

    rest = pl.ds(pl.multiple_of(other * half, half), half)
    for q in range(4):
        v_copy(q).wait_recv()
        amp_own[q, :, rest] = (amp_own[q, :, rest].astype(F32) - v_recv[q].astype(F32)).astype(BF16)

        @pl.when(diagonal)
        def _():
            amp_diag[q] = amp_own[q]
            amp_own[q] = jnp.zeros(amp_own.shape[1:], BF16)
            col_forward(q)

    @pl.when(jnp.logical_and(first, jnp.logical_not(diagonal)))
    def _():
        for q in range(4):
            row_copy(q, 0).wait_recv()
            row_forward(q)

    @pl.when(jnp.logical_not(diagonal))
    def _():
        for q in range(4):
            col_copy(q, 0).wait_recv()
            col_forward(q)

    @pl.when(jnp.logical_not(first))
    def _():
        for q in range(4):
            row_copy(q, 0).wait_recv()

    def both(ref, n):
        return ref[2 * n:2 * n + 2].reshape(2 * slots, 2 * half)

    cross = column ^ all_row
    for i in range(2):
        for j in range(2):
            g = occ[2 * I + i] ^ occ[2 * J + j]
            total = dot(both(int_own, j), both(amp_diag, i), 0, 0) + dot(both(int_diag, j), both(amp_own, i), 0, 0)
            total = jnp.where(cross == g, total, 0.0).astype(BF16)
            q = i * 2 + j
            for w in range(2):
                part[w, q] = dot(slot_of[w], total[w * half:(w + 1) * half], 1, 0).astype(BF16)
            part_copy(q).start()

    for q in range(4):
        part_copy(q).wait_recv()
        cycle = (part[h, q].astype(F32) + part_recv[q].astype(F32)).astype(BF16)
        for v in range(2):
            own[v, q] = cycle[:, v * half:(v + 1) * half]

        @pl.when(mid_self)
        def _():
            mid[h, q] = own[h, q]

        @pl.when(jnp.logical_not(mid_self))
        def _():
            hop_copy(q, h, h).start()

        hop_copy(q, other, h).start()

    for q in range(4):
        for v in (h, other):
            @pl.when(jnp.logical_not(jnp.logical_and(from_self, h == v)))
            def _():
                hop_copy(q, v, v).wait_recv()

            @pl.when(end_self)
            def _():
                mirrored[v, q] = mid[v, q]

            @pl.when(jnp.logical_not(end_self))
            def _():
                end_copy(q, v).start()

    for q in range(4):
        for v in range(2):
            @pl.when(jnp.logical_not(back_self))
            def _():
                end_copy(q, v).wait_recv()

    for q in range(4):
        v_copy(q).wait_send()
        part_copy(q).wait_send()
        for n, child in enumerate(col_child):
            @pl.when(child >= 0)
            def _():
                col_copy(q, n).wait_send()
        for n, (there, _) in enumerate(row_child):
            @pl.when(there)
            def _():
                row_copy(q, n).wait_send()
        for v in range(2):
            @pl.when(jnp.logical_not(jnp.logical_and(mid_self, h == v)))
            def _():
                hop_copy(q, v, v).wait_send()

            @pl.when(jnp.logical_not(end_self))
            def _():
                end_copy(q, v).wait_send()


def unpack_kernel(own, mirrored, slot_of, vir, occ, out):
    half = out.shape[3]
    I, J, h = lax.axis_index("row"), lax.axis_index("col"), lax.axis_index("vir")
    i, j = pl.program_id(0), pl.program_id(1)
    g = occ[2 * I + i] ^ occ[2 * J + j]
    here = pl.ds(pl.multiple_of(h * half, half), half)
    cross = column_of(vir[...]) ^ vir[:, here]
    for v in range(2):
        rows = slice(v * half, (v + 1) * half)
        left = jnp.concatenate([own[v, i * 2 + j], slot_of[:, rows]], axis=0)
        right = jnp.concatenate([slot_of[:, here], mirrored[v, j * 2 + i]], axis=0)
        out[0, 0, rows] = jnp.where(cross[rows] == g, dot(left, right, 0, 0), 0.0)


def packed_cycle(amplitudes, integrals, occ_irrep, vir_irrep):
    half = amplitudes.shape[3]
    full = 2 * half
    vmem = pl.BlockSpec(memory_space=pltpu.VMEM)
    smem = pl.BlockSpec(memory_space=pltpu.SMEM)
    vir = vir_irrep.reshape(1, full)
    tile = pltpu.VMEM((4, SLOTS, full), BF16)
    dma = pltpu.SemaphoreType.DMA
    halves = jax.ShapeDtypeStruct((2, 4, SLOTS, half), BF16)
    return pl.pallas_call(
        cycle_kernel,
        out_shape=[halves, halves, jax.ShapeDtypeStruct((SLOTS, full), BF16), jax.ShapeDtypeStruct((1, 1), F32)],
        in_specs=[pl.BlockSpec(memory_space=pl.ANY)] * 2 + [vmem, smem],
        out_specs=[vmem, vmem, vmem, vmem],
        scratch_shapes=[
            pltpu.VMEM(amplitudes.shape, BF16), pltpu.VMEM(integrals.shape, BF16), dma((2,)),
            tile, tile, tile, tile,
            pltpu.VMEM((4, SLOTS, half), BF16), pltpu.VMEM((4, SLOTS, half), BF16),
            pltpu.VMEM((2, 4, SLOTS, full), BF16), tile, pltpu.VMEM((2, 4, SLOTS, half), BF16),
            dma((4,)), dma((4,)), dma((5, 4)), dma((4,)), dma((5, 4)), dma((4,)), dma((4,)), dma((4,)),
            dma((2, 4)), dma((2, 4)), dma((2, 4)), dma((2, 4)),
        ],
        compiler_params=pltpu.CompilerParams(
            collective_id=0, has_side_effects=True, vmem_limit_bytes=32 * 2**20
        ),
    )(amplitudes, integrals, vir, occ_irrep)


def packed_sum(own, mirrored, slot_of, occ_irrep, vir_irrep):
    half = own.shape[3]
    full = 2 * half
    vmem = pl.BlockSpec(memory_space=pltpu.VMEM)
    smem = pl.BlockSpec(memory_space=pltpu.SMEM)
    return pl.pallas_call(
        unpack_kernel,
        grid=(2, 2),
        out_shape=jax.ShapeDtypeStruct((2, 2, full, half), F32),
        in_specs=[vmem, vmem, vmem, vmem, smem],
        out_specs=pl.BlockSpec((1, 1, full, half), lambda i, j: (i, j, 0, 0)),
        compiler_params=pltpu.CompilerParams(vmem_limit_bytes=32 * 2**20),
    )(own, mirrored, slot_of, vir_irrep.reshape(1, full), occ_irrep)


def from_diagonal(value, row_index, col_index, along):
    size = lax.axis_size("col")
    apart = (col_index - row_index if along == "col" else row_index - col_index) % size
    reach = 1
    while reach < size:
        pairs = []
        for near in range(size):
            for step in range(reach):
                source, target = (near + step) % size, (near + step + reach) % size
                if along == "col":
                    pairs.append((near * size + source, near * size + target))
                else:
                    pairs.append((source * size + near, target * size + near))
        moved = lax.ppermute(value, ("row", "col"), pairs)
        value = jnp.where(jnp.logical_and(apart >= reach, apart < 2 * reach), moved, value)
        reach *= 2
    return value


def from_other_half(value):
    return lax.ppermute(value, "vir", [(0, 1), (1, 0)])


def symmetry_mask(left, right, first, second):
    return (
        left[:, None, None, None]
        ^ right[None, :, None, None]
        ^ first[None, None, :, None]
        ^ second[None, None, None, :]
        == 0
    )


def contract(amplitude_tile, integral_tile):
    return jnp.einsum(
        "ikac,kjcb->ijab", amplitude_tile, integral_tile, preferred_element_type=jnp.float32
    )


def from_mirror(value):
    size = lax.axis_size("col")
    pairs = [(i * size + j, j * size + i) for i in range(size) for j in range(size)]
    return lax.ppermute(value, ("row", "col"), pairs)


def whole_plan(amplitudes, integrals, occ_irrep, vir_irrep):
    block_size = amplitudes.shape[0]
    virtual_count = amplitudes.shape[2]
    half_count = amplitudes.shape[3]
    row_index = lax.axis_index("row")
    col_index = lax.axis_index("col")
    half_index = lax.axis_index("vir")
    occ_row = lax.dynamic_slice_in_dim(occ_irrep, row_index * block_size, block_size)
    occ_col = lax.dynamic_slice_in_dim(occ_irrep, col_index * block_size, block_size)
    vir_half = lax.dynamic_slice_in_dim(vir_irrep, half_index * half_count, half_count)
    amp_masked = jnp.where(
        symmetry_mask(occ_row, occ_col, vir_irrep, vir_half), amplitudes, jnp.zeros_like(amplitudes)
    )
    int_masked = jnp.where(
        symmetry_mask(occ_row, occ_col, vir_half, vir_irrep), integrals, jnp.zeros_like(integrals)
    )
    flipped = lax.all_to_all(amp_masked, "vir", split_axis=2, concat_axis=3, tiled=True)
    combined = (
        2.0 * amp_masked.astype(jnp.float32)
        - jnp.transpose(flipped, (0, 1, 3, 2)).astype(jnp.float32)
    ).astype(jnp.bfloat16)
    off_diagonal = row_index != col_index
    empty_shape = (block_size, block_size, virtual_count, virtual_count)
    amp_row_diag = from_diagonal(combined, row_index, col_index, "col")
    int_col_diag = from_diagonal(int_masked, row_index, col_index, "row")
    own_term = contract(amp_row_diag, int_masked) + lax.cond(
        off_diagonal,
        lambda: contract(combined, int_col_diag),
        lambda: jnp.zeros(empty_shape, jnp.float32),
    )
    rounded = own_term.astype(jnp.bfloat16)
    kept = lax.dynamic_slice_in_dim(rounded, half_index * half_count, half_count, 3)
    moved = from_other_half(lax.dynamic_slice_in_dim(rounded, (1 - half_index) * half_count, half_count, 3))
    own_sum = (kept.astype(jnp.float32) + moved.astype(jnp.float32)).astype(jnp.bfloat16)
    facing = from_mirror(own_sum)
    paired = lax.all_to_all(facing, "vir", split_axis=2, concat_axis=3, tiled=True)
    return own_sum.astype(jnp.float32) + jnp.transpose(paired, (1, 0, 3, 2)).astype(jnp.float32)


def on_device(amplitudes, integrals, occ_irrep, vir_irrep):
    own, mirrored, slot_of, last_rank = packed_cycle(amplitudes, integrals, occ_irrep, vir_irrep)
    return lax.cond(
        last_rank[0, 0] < SLOTS,
        lambda: packed_sum(own, mirrored, slot_of, occ_irrep, vir_irrep),
        lambda: whole_plan(amplitudes, integrals, occ_irrep, vir_irrep),
    )


def solution(mesh):
    return jax.shard_map(
        on_device,
        mesh=mesh,
        in_specs=(P("row", "col", None, "vir"), P("row", "col", "vir", None), P(), P()),
        out_specs=P("row", "col", None, "vir"),
        check_vma=False,
    )
```

```python
import functools

import jax
import jax.numpy as jnp
from jax import lax
from jax.experimental import pallas as pl
from jax.experimental.pallas import tpu as pltpu
from jax.sharding import PartitionSpec as P

MESH = pl.DeviceIdType.MESH
LABELS = 8
SLOTS = 48
F32 = jnp.float32
BF16 = jnp.bfloat16

COL_TREE = (
    {0: 8, 8: 7, 4: 6, 12: 10, 1: 2, 15: 14},
    {0: 4, 8: 9, 4: 5, 12: 11},
    {0: 12, 4: 3, 12: 13},
    {0: 1},
    {0: 15},
)


def lookup(key, table, default):
    found = jnp.int32(default)
    for at, value in table.items():
        found = jnp.where(key == at, jnp.int32(value), found)
    return found


def dot(left, right, left_dim, right_dim):
    return lax.dot_general(left, right, (((left_dim,), (right_dim,)), ((), ())), preferred_element_type=F32)


def remote(src, dst, send_sem, recv_sem, device):
    return pltpu.make_async_remote_copy(
        src_ref=src, dst_ref=dst, send_sem=send_sem, recv_sem=recv_sem, device_id=device, device_id_type=MESH
    )


def column_of(row_labels):
    return jnp.broadcast_to(row_labels, (128, row_labels.shape[1])).T[:, :1]


def slot_matrix(labels, slots):
    count = labels.shape[1]
    is_label = (lax.broadcasted_iota(jnp.int32, (LABELS, count), 0) == labels).astype(F32)
    earlier = (
        lax.broadcasted_iota(jnp.int32, (count, count), 0) < lax.broadcasted_iota(jnp.int32, (count, count), 1)
    ).astype(F32)
    before = dot(is_label.astype(BF16), earlier.astype(BF16), 1, 0)
    rank = jnp.sum(before * is_label, axis=0, keepdims=True)
    slot = lax.broadcasted_iota(jnp.int32, (slots, count), 0).astype(F32)
    return jnp.where(slot == rank, 1.0, 0.0).astype(BF16), jnp.max(rank)


def cycle_kernel(
    amp_hbm, int_hbm, vir, occ, own, mirrored, slot_out, most_out,
    amp, itg, load_sem, amp_own, int_own, amp_diag, int_diag, v_send, v_recv, part, part_recv, mid,
    v_ss, v_rs, col_ss, col_rs, row_ss, row_rs, part_ss, part_rs, hop_ss, hop_rs, end_ss, end_rs,
):
    slots = SLOTS
    half = amp.shape[3]
    I, J, h = lax.axis_index("row"), lax.axis_index("col"), lax.axis_index("vir")
    other = 1 - h
    loads = [pltpu.make_async_copy(amp_hbm, amp, load_sem.at[0]), pltpu.make_async_copy(int_hbm, itg, load_sem.at[1])]
    for load in loads:
        load.start()
    diagonal = I == J
    partner = (I, J, other)

    apart = lax.rem(J - I + 16, 16)
    col_child = [lookup(apart, table, -1) for table in COL_TREE]
    col_parent = lookup(apart, {b: a for table in COL_TREE for a, b in table.items()}, 0)

    def along_col(offset):
        return (I, lax.rem(I + offset + 16, 16), h)

    dy = lax.rem(I // 8 + J // 8, 2)
    dx = lax.rem(lax.rem(I // 2, 4) - lax.rem(J // 2, 4) + 4, 4)
    dc = lax.rem(I + J, 2)

    def at_plane(y, x, core):
        row = lax.rem(J // 8 + y, 2) * 8 + lax.rem(lax.rem(J // 2, 4) + x, 4) * 2 + lax.rem(J + core, 2)
        return (row, J, h)

    first = dc == 0
    row_child = [
        (first, at_plane(dy, dx, 1)),
        (jnp.logical_and(first, dx == 0), at_plane(dy, 2, 0)),
        (jnp.logical_and(first, dx == 0), at_plane(dy, 3, 0)),
        (jnp.logical_and(first, dx == 0), at_plane(dy, 1, 0)),
        (jnp.logical_and(first, dx + dy == 0), at_plane(1, 0, 0)),
    ]
    parent_y = jnp.where(jnp.logical_and(first, dx == 0), 0, dy)
    parent_x = jnp.where(first, 0, dx)
    row_parent = at_plane(parent_y, parent_x, 0)

    r, s = I // 2, J // 2
    mid_row = lax.rem(5 * r + s, 8) * 2 + lax.rem(I, 2)
    from_row = lax.rem(5 * (r - s + 8), 8) * 2 + lax.rem(I, 2)
    back_row = lax.rem(5 * s + r, 8) * 2 + lax.rem(J, 2)
    mid_self = mid_row == I
    from_self = from_row == I
    end_self = jnp.logical_and(from_row == J, I == J)
    end_at = (J, from_row, h)

    barrier = pltpu.get_barrier_semaphore()

    def greet(device):
        pl.semaphore_signal(barrier, inc=1, device_id=device, device_id_type=MESH)

    greet(partner)

    @pl.when(jnp.logical_not(diagonal))
    def _():
        greet(along_col(col_parent))
        greet(row_parent)

    for v in range(2):
        @pl.when(jnp.logical_not(jnp.logical_and(from_self, h == v)))
        def _():
            greet((from_row, J, v))

    back_self = jnp.logical_and(back_row == I, I == J)

    @pl.when(jnp.logical_not(back_self))
    def _():
        greet((back_row, I, h))

    labels = [vir[:, w * half:(w + 1) * half] for w in range(2)]
    labels_here = jnp.where(h == 0, labels[0], labels[1])
    (slot_low, most_low), (slot_high, most_high) = [slot_matrix(labels[w], slots) for w in range(2)]
    slot_of = [slot_low, slot_high]
    most_out[...] = jnp.full((1, 1), jnp.maximum(most_low, most_high), F32)
    for w in range(2):
        slot_out[:, w * half:(w + 1) * half] = slot_of[w]
    slot_here = jnp.where(h == 0, slot_of[0].astype(F32), slot_of[1].astype(F32)).astype(BF16)
    column = column_of(vir[...])
    column_here = jnp.where(h == 0, column[:half], column[half:])
    all_row = vir[...]

    for load in loads:
        load.wait()
    cross_amp = column ^ labels_here
    cross_int = column_here ^ all_row
    for i in range(2):
        for k in range(2):
            g = occ[2 * I + i] ^ occ[2 * J + k]
            kept = jnp.where(cross_amp == g, amp[i, k].astype(F32), 0.0).astype(BF16)
            packed = dot(slot_here, kept, 1, 1)
            flipped = [dot(slot_of[w], kept[w * half:(w + 1) * half], 1, 0) for w in range(2)]
            flipped_here = jnp.where(h == 0, flipped[0], flipped[1])
            v_send[i * 2 + k] = jnp.where(h == 0, flipped[1], flipped[0]).astype(BF16)
            for w in range(2):
                piece = 2.0 * packed[:, w * half:(w + 1) * half]
                amp_own[i * 2 + k, :, w * half:(w + 1) * half] = jnp.where(h == w, piece - flipped_here, piece).astype(BF16)
            kept_int = jnp.where(cross_int == g, itg[i, k].astype(F32), 0.0).astype(BF16)
            int_own[k * 2 + i] = dot(slot_here, kept_int, 1, 0).astype(BF16)

    expected = jnp.int32(1)
    for child in col_child:
        expected += jnp.where(child >= 0, 1, 0)
    for there, _ in row_child:
        expected += jnp.where(there, 1, 0)
    expected += jnp.where(mid_self, 1, 2)
    expected += jnp.where(end_self, 0, 1)
    pl.semaphore_wait(barrier, expected)

    def v_copy(q):
        return remote(v_send.at[q], v_recv.at[q], v_ss.at[q], v_rs.at[q], partner)

    def col_copy(q, n):
        return remote(amp_diag.at[q], amp_diag.at[q], col_ss.at[n, q], col_rs.at[q], along_col(col_child[n]))

    def row_copy(q, n):
        return remote(int_diag.at[q], int_diag.at[q], row_ss.at[n, q], row_rs.at[q], row_child[n][1])

    def part_copy(q):
        return remote(part.at[other, q], part_recv.at[q], part_ss.at[q], part_rs.at[q], partner)

    def hop_copy(q, v, slot):
        return remote(own.at[v, q], mid.at[slot, q], hop_ss.at[v, q], hop_rs.at[slot, q], (mid_row, J, v))

    def end_copy(q, v):
        return remote(mid.at[v, q], mirrored.at[v, q], end_ss.at[v, q], end_rs.at[v, q], end_at)

    for q in range(4):
        v_copy(q).start()

    @pl.when(diagonal)
    def _():
        int_diag[...] = int_own[...]

    def row_forward(q):
        for n, (there, _) in reversed(list(enumerate(row_child))):
            @pl.when(there)
            def _():
                row_copy(q, n).start()

    def col_forward(q):
        for n, child in enumerate(col_child):
            @pl.when(child >= 0)
            def _():
                col_copy(q, n).start()

    @pl.when(diagonal)
    def _():
        for q in range(4):
            row_forward(q)

    rest = pl.ds(pl.multiple_of(other * half, half), half)
    for q in range(4):
        v_copy(q).wait_recv()
        amp_own[q, :, rest] = (amp_own[q, :, rest].astype(F32) - v_recv[q].astype(F32)).astype(BF16)

        @pl.when(diagonal)
        def _():
            amp_diag[q] = amp_own[q]
            amp_own[q] = jnp.zeros(amp_own.shape[1:], BF16)
            col_forward(q)

    @pl.when(jnp.logical_and(first, jnp.logical_not(diagonal)))
    def _():
        for q in range(4):
            row_copy(q, 0).wait_recv()
            row_forward(q)

    @pl.when(jnp.logical_not(diagonal))
    def _():
        for q in range(4):
            col_copy(q, 0).wait_recv()
            col_forward(q)

    @pl.when(jnp.logical_not(first))
    def _():
        for q in range(4):
            row_copy(q, 0).wait_recv()

    def both(ref, n):
        return ref[2 * n:2 * n + 2].reshape(2 * slots, 2 * half)

    cross = column ^ all_row
    for i in range(2):
        for j in range(2):
            g = occ[2 * I + i] ^ occ[2 * J + j]
            total = dot(both(int_own, j), both(amp_diag, i), 0, 0) + dot(both(int_diag, j), both(amp_own, i), 0, 0)
            total = jnp.where(cross == g, total, 0.0).astype(BF16)
            q = i * 2 + j
            for w in range(2):
                part[w, q] = dot(slot_of[w], total[w * half:(w + 1) * half], 1, 0).astype(BF16)
            part_copy(q).start()

    for q in range(4):
        part_copy(q).wait_recv()
        cycle = (part[h, q].astype(F32) + part_recv[q].astype(F32)).astype(BF16)
        for v in range(2):
            own[v, q] = cycle[:, v * half:(v + 1) * half]

        @pl.when(mid_self)
        def _():
            mid[h, q] = own[h, q]

        @pl.when(jnp.logical_not(mid_self))
        def _():
            hop_copy(q, h, h).start()

        hop_copy(q, other, h).start()

    for q in range(4):
        for v in (h, other):
            @pl.when(jnp.logical_not(jnp.logical_and(from_self, h == v)))
            def _():
                hop_copy(q, v, v).wait_recv()

            @pl.when(end_self)
            def _():
                mirrored[v, q] = mid[v, q]

            @pl.when(jnp.logical_not(end_self))
            def _():
                end_copy(q, v).start()

    for q in range(4):
        for v in range(2):
            @pl.when(jnp.logical_not(back_self))
            def _():
                end_copy(q, v).wait_recv()

    for q in range(4):
        v_copy(q).wait_send()
        part_copy(q).wait_send()
        for n, child in enumerate(col_child):
            @pl.when(child >= 0)
            def _():
                col_copy(q, n).wait_send()
        for n, (there, _) in enumerate(row_child):
            @pl.when(there)
            def _():
                row_copy(q, n).wait_send()
        for v in range(2):
            @pl.when(jnp.logical_not(jnp.logical_and(mid_self, h == v)))
            def _():
                hop_copy(q, v, v).wait_send()

            @pl.when(jnp.logical_not(end_self))
            def _():
                end_copy(q, v).wait_send()


def unpack_kernel(own, mirrored, slot_of, vir, occ, out):
    half = out.shape[3]
    I, J, h = lax.axis_index("row"), lax.axis_index("col"), lax.axis_index("vir")
    i, j = pl.program_id(0), pl.program_id(1)
    g = occ[2 * I + i] ^ occ[2 * J + j]
    here = pl.ds(pl.multiple_of(h * half, half), half)
    cross = column_of(vir[...]) ^ vir[:, here]
    for v in range(2):
        rows = slice(v * half, (v + 1) * half)
        left = jnp.concatenate([own[v, i * 2 + j], slot_of[:, rows]], axis=0)
        right = jnp.concatenate([slot_of[:, here], mirrored[v, j * 2 + i]], axis=0)
        out[0, 0, rows] = jnp.where(cross[rows] == g, dot(left, right, 0, 0), 0.0)


def packed_cycle(amplitudes, integrals, occ_irrep, vir_irrep):
    half = amplitudes.shape[3]
    full = 2 * half
    vmem = pl.BlockSpec(memory_space=pltpu.VMEM)
    smem = pl.BlockSpec(memory_space=pltpu.SMEM)
    vir = vir_irrep.reshape(1, full)
    tile = pltpu.VMEM((4, SLOTS, full), BF16)
    dma = pltpu.SemaphoreType.DMA
    halves = jax.ShapeDtypeStruct((2, 4, SLOTS, half), BF16)
    return pl.pallas_call(
        cycle_kernel,
        out_shape=[halves, halves, jax.ShapeDtypeStruct((SLOTS, full), BF16), jax.ShapeDtypeStruct((1, 1), F32)],
        in_specs=[pl.BlockSpec(memory_space=pl.ANY)] * 2 + [vmem, smem],
        out_specs=[vmem, vmem, vmem, vmem],
        scratch_shapes=[
            pltpu.VMEM(amplitudes.shape, BF16), pltpu.VMEM(integrals.shape, BF16), dma((2,)),
            tile, tile, tile, tile,
            pltpu.VMEM((4, SLOTS, half), BF16), pltpu.VMEM((4, SLOTS, half), BF16),
            pltpu.VMEM((2, 4, SLOTS, full), BF16), tile, pltpu.VMEM((2, 4, SLOTS, half), BF16),
            dma((4,)), dma((4,)), dma((5, 4)), dma((4,)), dma((5, 4)), dma((4,)), dma((4,)), dma((4,)),
            dma((2, 4)), dma((2, 4)), dma((2, 4)), dma((2, 4)),
        ],
        compiler_params=pltpu.CompilerParams(
            collective_id=0, has_side_effects=True, vmem_limit_bytes=32 * 2**20
        ),
    )(amplitudes, integrals, vir, occ_irrep)


def packed_sum(own, mirrored, slot_of, occ_irrep, vir_irrep):
    half = own.shape[3]
    full = 2 * half
    vmem = pl.BlockSpec(memory_space=pltpu.VMEM)
    smem = pl.BlockSpec(memory_space=pltpu.SMEM)
    return pl.pallas_call(
        unpack_kernel,
        grid=(2, 2),
        out_shape=jax.ShapeDtypeStruct((2, 2, full, half), F32),
        in_specs=[vmem, vmem, vmem, vmem, smem],
        out_specs=pl.BlockSpec((1, 1, full, half), lambda i, j: (i, j, 0, 0)),
        compiler_params=pltpu.CompilerParams(vmem_limit_bytes=32 * 2**20),
    )(own, mirrored, slot_of, vir_irrep.reshape(1, full), occ_irrep)


def from_diagonal(value, row_index, col_index, along):
    size = lax.axis_size("col")
    apart = (col_index - row_index if along == "col" else row_index - col_index) % size
    reach = 1
    while reach < size:
        pairs = []
        for near in range(size):
            for step in range(reach):
                source, target = (near + step) % size, (near + step + reach) % size
                if along == "col":
                    pairs.append((near * size + source, near * size + target))
                else:
                    pairs.append((source * size + near, target * size + near))
        moved = lax.ppermute(value, ("row", "col"), pairs)
        value = jnp.where(jnp.logical_and(apart >= reach, apart < 2 * reach), moved, value)
        reach *= 2
    return value


def from_other_half(value):
    return lax.ppermute(value, "vir", [(0, 1), (1, 0)])


def symmetry_mask(left, right, first, second):
    return (
        left[:, None, None, None]
        ^ right[None, :, None, None]
        ^ first[None, None, :, None]
        ^ second[None, None, None, :]
        == 0
    )


def contract(amplitude_tile, integral_tile):
    return jnp.einsum(
        "ikac,kjcb->ijab", amplitude_tile, integral_tile, preferred_element_type=jnp.float32
    )


def from_mirror(value):
    size = lax.axis_size("col")
    pairs = [(i * size + j, j * size + i) for i in range(size) for j in range(size)]
    return lax.ppermute(value, ("row", "col"), pairs)


def whole_plan(amplitudes, integrals, occ_irrep, vir_irrep):
    block_size = amplitudes.shape[0]
    virtual_count = amplitudes.shape[2]
    half_count = amplitudes.shape[3]
    row_index = lax.axis_index("row")
    col_index = lax.axis_index("col")
    half_index = lax.axis_index("vir")
    occ_row = lax.dynamic_slice_in_dim(occ_irrep, row_index * block_size, block_size)
    occ_col = lax.dynamic_slice_in_dim(occ_irrep, col_index * block_size, block_size)
    vir_half = lax.dynamic_slice_in_dim(vir_irrep, half_index * half_count, half_count)
    amp_masked = jnp.where(
        symmetry_mask(occ_row, occ_col, vir_irrep, vir_half), amplitudes, jnp.zeros_like(amplitudes)
    )
    int_masked = jnp.where(
        symmetry_mask(occ_row, occ_col, vir_half, vir_irrep), integrals, jnp.zeros_like(integrals)
    )
    flipped = lax.all_to_all(amp_masked, "vir", split_axis=2, concat_axis=3, tiled=True)
    combined = (
        2.0 * amp_masked.astype(jnp.float32)
        - jnp.transpose(flipped, (0, 1, 3, 2)).astype(jnp.float32)
    ).astype(jnp.bfloat16)
    off_diagonal = row_index != col_index
    empty_shape = (block_size, block_size, virtual_count, virtual_count)
    amp_row_diag = from_diagonal(combined, row_index, col_index, "col")
    int_col_diag = from_diagonal(int_masked, row_index, col_index, "row")
    own_term = contract(amp_row_diag, int_masked) + lax.cond(
        off_diagonal,
        lambda: contract(combined, int_col_diag),
        lambda: jnp.zeros(empty_shape, jnp.float32),
    )
    rounded = own_term.astype(jnp.bfloat16)
    kept = lax.dynamic_slice_in_dim(rounded, half_index * half_count, half_count, 3)
    moved = from_other_half(lax.dynamic_slice_in_dim(rounded, (1 - half_index) * half_count, half_count, 3))
    own_sum = (kept.astype(jnp.float32) + moved.astype(jnp.float32)).astype(jnp.bfloat16)
    facing = from_mirror(own_sum)
    paired = lax.all_to_all(facing, "vir", split_axis=2, concat_axis=3, tiled=True)
    return own_sum.astype(jnp.float32) + jnp.transpose(paired, (1, 0, 3, 2)).astype(jnp.float32)


def on_device(amplitudes, integrals, occ_irrep, vir_irrep):
    own, mirrored, slot_of, last_rank = packed_cycle(amplitudes, integrals, occ_irrep, vir_irrep)
    return lax.cond(
        last_rank[0, 0] < SLOTS,
        lambda: packed_sum(own, mirrored, slot_of, occ_irrep, vir_irrep),
        lambda: whole_plan(amplitudes, integrals, occ_irrep, vir_irrep),
    )


def solution(mesh):
    return jax.shard_map(
        on_device,
        mesh=mesh,
        in_specs=(P("row", "col", None, "vir"), P("row", "col", "vir", None), P(), P()),
        out_specs=P("row", "col", None, "vir"),
        check_vma=False,
    )
```
